128 devices in a mesh: dp: 32 (over y, z, core), expert: 4 (over x).
Axes of the slice: x: 4, y: 4, z: 4, core: 2. Of those that a mesh axis runs over, the one named last changes fastest.
Arguments:
- tokens: bfloat16 [768, 4096], P(('dp', 'expert')), may hold values from -6 to 6
- cotangent: bfloat16 [768, 4096], P(('dp', 'expert')), may hold values from -2 to 2
- route_ids: int32 [768, 2], P(('dp', 'expert')), may hold values from 0 to 3, all different within a row; in each aligned block of 6 rows (0 to 5, 6 to 11, ...) at most 4 rows name the same one
- gate_values: bfloat16 [768, 2], P(('dp', 'expert')), may hold values from 0.19921875 to 1
- gate_weight: bfloat16 [4, 4096, 14336], P('expert', None, 'dp'), may hold values from -0.09375 to 0.09375
- up_weight: bfloat16 [4, 4096, 14336], P('expert', None, 'dp'), may hold values from -0.09375 to 0.09375
- down_weight: bfloat16 [4, 14336, 4096], P('expert', 'dp'), may hold values from -0.046875 to 0.046875
- gate_direction: bfloat16 [4, 4096, 14336], P('expert', None, 'dp'), may hold values from -0.09375 to 0.09375
- up_direction: bfloat16 [4, 4096, 14336], P('expert', None, 'dp'), may hold values from -0.09375 to 0.09375
Outputs:
- gate_curvature: bfloat16 [4, 4096, 14336], P('expert', None, 'dp')
- up_curvature: bfloat16 [4, 4096, 14336], P('expert', None, 'dp')
The draws below stay inside these ranges and needn't reach their ends.
Inputs may be any that keep to these rules, and one draw needn't show every extreme that they name: `route_ids`: the two ids of a row differ. In the rows of one device (aligned blocks of 6 rows) no expert is named more than 4 times, a bound that some block reaches.
All inputs are finite; a program needn't handle non-finite values.
Results may differ from the reference program's by a relative error of at most 0.0057.
Values may be sent and summed in bfloat16 or wider, within the bound.
A program may use at most 128 MiB of HBM per device.

```python
import math
import jax
import jax.numpy as jnp
import numpy as np
from jax import lax

D = 4096
FF = 14336
TOP = 2
TOK_DEV = 6
EXPERTS = 4
CAP = 4
TOKENS = 768
N_DP = 32
N_EXPERT = 4


def shard_levels(rng, shape, cuts, smallest, largest):
    def one(axis_at, parts):
        steps = jax.random.uniform(jax.random.fold_in(jax.random.fold_in(rng, 6), axis_at), (parts,), jnp.float32, smallest / len(cuts), largest / len(cuts))
        return jnp.repeat(jnp.exp(steps), shape[axis_at] // parts).reshape((-1,) + (1,) * (len(shape) - axis_at - 1))

    loudness = one(*cuts[0])
    for cut in cuts[1:]:
        loudness = loudness * one(*cut)
    return loudness


def deal_out(key, own, number, rows, number_of, top, limit, slope):
    ranking = jax.random.permutation(key, number_of)
    packed, usual = portions_of(number_of, rows * top, limit, slope, True), portions_of(number_of, rows * top, limit, slope, False)
    places = jnp.arange(number_of)

    def named(sizes, turn):
        used = int((sizes > 0).sum())
        fixed = max(1, used // 4)
        moved = fixed + (places - fixed + turn * (used - fixed)) % max(1, number_of - fixed)
        return jnp.zeros((number_of,), jnp.int32).at[ranking[jnp.where(places < fixed, places, moved)]].set(jnp.asarray(sizes, jnp.int32))

    sizes = jnp.where(number % 4 == 0, named(packed, number // 4), named(usual, number - number // 4 - 1))
    mixed = jax.random.permutation(jax.random.fold_in(own, 3), number_of)
    giver, sink = mixed[0:number_of // 2 * 2:2], mixed[1:number_of // 2 * 2:2]
    margin = jnp.minimum(sizes[giver] - 1, limit - sizes[sink]) // 2
    margin = jnp.where((giver == ranking[0]) | (sink == ranking[0]) | (sizes[sink] == 0), 0, jnp.maximum(margin, 0))
    moved = jax.random.randint(jax.random.fold_in(own, 4), (number_of // 2,), 0, 1 << 20) % (margin + 1)
    sizes = sizes.at[giver].add(-moved).at[sink].add(moved)
    items = jnp.searchsorted(jnp.cumsum(sizes), jnp.arange(rows * top), side="right").astype(jnp.int32)
    grid = items.reshape(top, rows).T
    grid = grid[jax.random.permutation(jax.random.fold_in(own, 1), rows)]
    turn = jax.random.randint(jax.random.fold_in(own, 2), (rows, 1), 0, top)
    return jnp.take_along_axis(grid, (jnp.arange(top)[None, :] + turn) % top, axis=1)


def portions_of(number_of, total, most, lean, full):
    loads = [(1 << 20) // math.isqrt(grade ** lean) + 1 for grade in range(1, number_of + 1)]
    largest = most if full else min(most, max(-(-total // number_of), total * loads[0] // sum(loads)))
    least = 1 if total - largest >= number_of - 1 else 0
    holding, rest = [largest] + [least] * (number_of - 1), total - largest - least * (number_of - 1)
    while rest > 0:
        candidates = [i for i in range(1, number_of) if holding[i] < largest] or [i for i in range(1, number_of) if holding[i] < most]
        pool, budget = sum([loads[i] for i in candidates]), rest
        for i in candidates:
            addition = min(most - holding[i], max(1, budget * loads[i] // pool), rest)
            holding[i] = holding[i] + addition
            rest = rest - addition
    return np.array(holding)


def gaussian(key, extent, scale, most, cuts=(), kind=jnp.bfloat16):
    array = scale * jax.random.normal(key, extent, jnp.float32)
    if cuts:
        array = array * shard_levels(key, extent, cuts, -0.22, 0.18)
    return jnp.clip(array, -most, most).astype(kind)


def setup_inputs(seed: int = 0) -> dict:
    arg_keys = jax.random.split(jax.random.key(seed), 10)
    tokens = gaussian(arg_keys[0], (TOKENS, D), 1.0, 6.0, ((0, 128),))
    cotangent = gaussian(arg_keys[1], (TOKENS, D), (4.0 / TOKENS ** 0.5), 2.0, ((0, 128),))
    route_ids_keys = jax.random.split(jax.random.fold_in(arg_keys[2], 1), TOKENS // TOK_DEV)
    route_ids_turns = jax.random.permutation(jax.random.fold_in(arg_keys[2], 3), TOKENS // TOK_DEV)
    route_ids = jax.vmap(lambda own, number: deal_out(jax.random.fold_in(arg_keys[2], 2), own, number, TOK_DEV, EXPERTS, TOP, CAP, 2))(route_ids_keys, route_ids_turns).reshape((TOKENS, TOP))
    gate_values = jnp.clip(0.19921875 + 0.80078125 * jax.random.uniform(arg_keys[3], (TOKENS, TOP), jnp.float32) ** shard_levels(arg_keys[3], (TOKENS, TOP), ((0, 128),), -0.2, 0.2), 0.19921875, 1.0).astype(jnp.bfloat16)
    gate_weight = gaussian(arg_keys[4], (EXPERTS, D, FF), D ** -0.5, 0.09375, ((0, 4), (2, 32)))
    up_weight = gaussian(arg_keys[5], (EXPERTS, D, FF), D ** -0.5, 0.09375, ((0, 4), (2, 32)))
    down_weight = gaussian(arg_keys[6], (EXPERTS, FF, D), FF ** -0.5, 0.046875, ((0, 4), (1, 32)))
    gate_direction = gaussian(arg_keys[7], (EXPERTS, D, FF), D ** -0.5, 0.09375, ((0, 4), (2, 32)))
    up_direction = gaussian(arg_keys[8], (EXPERTS, D, FF), D ** -0.5, 0.09375, ((0, 4), (2, 32)))
    return dict(tokens=tokens, cotangent=cotangent, route_ids=route_ids, gate_values=gate_values, gate_weight=gate_weight, up_weight=up_weight, down_weight=down_weight, gate_direction=gate_direction, up_direction=up_direction)


def slopes(pre):
    sig = jax.nn.sigmoid(pre)
    first = sig * (1.0 + pre * (1.0 - sig))
    second = sig * (1.0 - sig) * (2.0 + pre * (1.0 - 2.0 * sig))
    return first, second


def curvature(rows_x, rows_g, w_gate, w_up, w_down, d_gate, d_up):
    gate_pre = jnp.dot(rows_x, w_gate, preferred_element_type=jnp.float32)
    up_pre = jnp.dot(rows_x, w_up, preferred_element_type=jnp.float32)
    gate_tan = jnp.dot(rows_x, d_gate, preferred_element_type=jnp.float32)
    up_tan = jnp.dot(rows_x, d_up, preferred_element_type=jnp.float32)
    hidden_grad = lax.dot_general(rows_g, w_down, (((1,), (1,)), ((), ())), preferred_element_type=jnp.float32)
    first, second = slopes(gate_pre)
    gate_term = (hidden_grad * (second * gate_tan * up_pre + first * up_tan)).astype(jnp.bfloat16)
    up_term = (hidden_grad * first * gate_tan).astype(jnp.bfloat16)
    gate_sum = lax.dot_general(rows_x, gate_term, (((0,), (0,)), ((), ())), preferred_element_type=jnp.float32)
    up_sum = lax.dot_general(rows_x, up_term, (((0,), (0,)), ((), ())), preferred_element_type=jnp.float32)
    return gate_sum, up_sum


def reference(tokens, cotangent, route_ids, gate_values, gate_weight, up_weight, down_weight, gate_direction, up_direction):
    row_count = N_DP * N_EXPERT * CAP
    positions = jnp.arange(TOKENS, dtype=jnp.int32)

    def one_expert(items):
        expert_id, w_gate, w_up, w_down, d_gate, d_up = items
        matches = route_ids == expert_id
        weight = jnp.sum(jnp.where(matches, gate_values.astype(jnp.float32), jnp.float32(0.0)), axis=1)
        routed = jnp.any(matches, axis=1)
        sort_key = jnp.where(routed, 0, TOKENS).astype(jnp.int32) + positions
        order = jnp.argsort(sort_key)[:row_count].astype(jnp.int32)
        rows_x = tokens[order]
        rows_g = (weight[order][:, None] * cotangent[order].astype(jnp.float32)).astype(jnp.bfloat16)
        return curvature(rows_x, rows_g, w_gate, w_up, w_down, d_gate, d_up)

    expert_ids = jnp.arange(EXPERTS, dtype=jnp.int32)
    gate_sum, up_sum = lax.map(one_expert, (expert_ids, gate_weight, up_weight, down_weight, gate_direction, up_direction))
    return gate_sum.astype(jnp.bfloat16), up_sum.astype(jnp.bfloat16)
```

```python
import functools

import jax
import jax.numpy as jnp
from jax import lax
from jax.experimental import pallas as pl
from jax.experimental.pallas import tpu as pltpu
from jax.sharding import PartitionSpec as P

MESH = pl.DeviceIdType.MESH
NT = (((1,), (1,)), ((), ()))
TN = (((0,), (0,)), ((), ()))
META = 128
CHUNKS = 8
VMEM_LIMIT = 56 * 2**20


def dispatch_matrix(ids, gates, ring):
    row = lax.broadcasted_iota(jnp.int32, (16, 128), 0)
    lane = lax.broadcasted_iota(jnp.int32, (16, 128), 1)
    expert = lane >> 5
    kind = (lane >> 4) & 1
    here = (((lane >> 2) & 3) == ring) & ((row >> 3) == kind)
    slot = lane & 3
    taken = jnp.zeros((16, 128), jnp.int32)
    out = jnp.zeros((16, 128), jnp.float32)
    for t in range(ids.shape[1]):
        first = jnp.broadcast_to(ids[0:1, t : t + 1], (16, 128)) == expert
        second = jnp.broadcast_to(ids[1:2, t : t + 1], (16, 128)) == expert
        gate = jnp.where(
            first,
            jnp.broadcast_to(gates[0:1, t : t + 1], (16, 128)),
            jnp.broadcast_to(gates[1:2, t : t + 1], (16, 128)),
        )
        routed = first | second
        value = jnp.where(kind == 0, jnp.float32(1.0), gate)
        hit = routed & here & (taken == slot) & ((row & 7) == t)
        out = jnp.where(hit, value, out)
        taken = taken + routed.astype(jnp.int32)
    return out.astype(jnp.bfloat16)


def front(
    tok,
    cot,
    ids,
    gates,
    wg,
    wu,
    dg,
    du,
    wd,
    xout,
    terms,
    raw,
    outbox,
    rows,
    weights,
    acc,
    raw_send,
    raw_recv,
    x_send,
    x_recv,
    ring_send,
    ring_recv,
    half_send,
    half_recv,
    sib_send,
    sib_recv,
    w_sem,
    xout_sem,
):
    n = CHUNKS
    width = tok.shape[1] // n
    hidden = wg.shape[0]
    dp = lax.axis_index("dp")
    x = lax.axis_index("expert")
    y, z, core = dp // 8, (dp // 2) % 4, dp % 2
    q = jnp.where(core == 0, y, z)
    r = jnp.where(core == 0, z, y)

    def plane(q_at, r_at, c_at):
        q_at, r_at = lax.rem(q_at, 4), lax.rem(r_at, 4)
        y_at = jnp.where(core == 0, q_at, r_at)
        z_at = jnp.where(core == 0, r_at, q_at)
        return (y_at * 4 + z_at) * 2 + c_at

    raw_to = [(plane(q + d, r, core), x) for d in (1, 3, 2)]
    x_to = [(dp, lax.rem(x + d, 4)) for d in (1, 3, 2)]
    ring_to = [(plane(q, r + d, core), x) for d in (1, 3)]
    sibling = (dp + 1 - 2 * core, x)

    barrier = pltpu.get_barrier_semaphore()
    partners = raw_to + x_to + ring_to + [sibling]
    for device in partners:
        pl.semaphore_signal(barrier, inc=1, device_id=device, device_id_type=MESH)

    def weight_copies(k):
        return [
            pltpu.make_async_copy(
                w.at[:, pl.ds(pl.multiple_of(k * width, width), width)],
                weights.at[k, j],
                w_sem.at[k],
            )
            for j, w in enumerate((wg, wu, dg, du, wd))
        ]

    raw[q] = jnp.zeros(raw.shape[1:], raw.dtype)
    raw[q, 0:6, META:] = tok[...]
    raw[q, 8:14, META:] = cot[...]
    raw[q, :, 0:META] = dispatch_matrix(ids[...], gates[...].astype(jnp.float32), q)

    pl.semaphore_wait(barrier, len(partners))

    def raw_columns(k):
        if k == 0:
            return pl.ds(0, META + width)
        return pl.ds(META + k * width, width)

    def raw_copy(k, i, source):
        return pltpu.make_async_remote_copy(
            src_ref=raw.at[q, :, raw_columns(k)],
            dst_ref=raw.at[source, :, raw_columns(k)],
            send_sem=raw_send.at[i],
            recv_sem=raw_recv.at[k, i],
            device_id=raw_to[i],
            device_id_type=MESH,
        )

    for k in range(n):
        for i in range(3):
            raw_copy(k, i, q).start()

    @pl.loop(0, n)
    def _(k):
        for copy in weight_copies(k):
            copy.start()

    acc[...] = jnp.zeros_like(acc)

    def x_copy(k, i):
        to = lax.rem(x + (1, 3, 2)[i], 4)
        return pltpu.make_async_remote_copy(
            src_ref=outbox.at[k, to],
            dst_ref=rows.at[k, :, core, r, x],
            send_sem=x_send.at[i],
            recv_sem=x_recv.at[k, i],
            device_id=x_to[i],
            device_id_type=MESH,
        )

    def select(k):
        columns = pl.ds(pl.multiple_of(META + k * width, 128), width)
        blocks = raw[:, :, columns].reshape(64, width)
        matrix = raw[:, :, 0:META].reshape(64, META)
        slots = lax.dot_general(matrix, blocks, TN, preferred_element_type=jnp.float32)
        slots = slots.astype(jnp.bfloat16).reshape(4, 2, 16, width)
        outbox[k] = slots
        rows[k, :, core, r, x] = outbox[k, x]
        for i in range(3):
            x_copy(k, i).start()

    left, right, across = lax.rem(r + 3, 4), lax.rem(r + 1, 4), lax.rem(r + 2, 4)

    def ring_copy(k, i):
        return pltpu.make_async_remote_copy(
            src_ref=rows.at[k, :, core, r],
            dst_ref=rows.at[k, :, core, r],
            send_sem=ring_send.at[i],
            recv_sem=ring_recv.at[k, i],
            device_id=ring_to[i],
            device_id_type=MESH,
        )

    def half_copy(k, i):
        at = left if i == 0 else right
        return pltpu.make_async_remote_copy(
            src_ref=rows.at[k, i, core, at],
            dst_ref=rows.at[k, i, core, at],
            send_sem=half_send.at[i],
            recv_sem=half_recv.at[k, i],
            device_id=ring_to[i],
            device_id_type=MESH,
        )

    def sib_copy(k, i):
        at = (r, left, right, across)[i]
        return pltpu.make_async_remote_copy(
            src_ref=rows.at[k, :, core, at],
            dst_ref=rows.at[k, :, core, at],
            send_sem=sib_send.at[i],
            recv_sem=sib_recv.at[k, i],
            device_id=sibling,
            device_id_type=MESH,
        )

    def xout_copy(k):
        return pltpu.make_async_copy(rows.at[k, 0], xout.at[k], xout_sem)

    for k in range(n):
        for i in range(3):
            raw_copy(k, i, q).wait_recv()
        select(k)

    def exchange(k):
        for i in range(3):
            x_copy(k, i).wait_recv()
        for i in range(2):
            ring_copy(k, i).start()
        sib_copy(k, 0).start()

    def forward(k):
        for i in range(2):
            ring_copy(k, i).wait_recv()
        for i in range(2):
            half_copy(k, i).start()
        for i in (1, 2):
            sib_copy(k, i).start()

    def finish(k):
        for i in range(2):
            half_copy(k, i).wait_recv()
        sib_copy(k, 3).start()

    def compute(k):
        for i in range(4):
            sib_copy(k, i).wait_recv()
        xout_copy(k).start()
        pltpu.make_async_copy(weights.at[k], weights.at[k], w_sem.at[k]).wait()
        for j in range(5):
            part = rows[k, j // 4].reshape(512, width)
            acc[j] += lax.dot_general(
                weights[k, j], part, NT, preferred_element_type=jnp.float32
            )

    @pl.loop(0, n + 4)
    def _(i):
        @pl.when(i < n)
        def _():
            exchange(i)

        @pl.when((i >= 2) & (i < n + 2))
        def _():
            forward(i - 2)

        @pl.when((i >= 3) & (i < n + 3))
        def _():
            finish(i - 3)

        @pl.when(i >= 4)
        def _():
            compute(i - 4)

    @pl.loop(0, hidden // 16)
    def _(b):
        at = pl.ds(pl.multiple_of(b * 16, 16), 16)
        gate_pre, up_pre, gate_tan, up_tan = [acc[j, at, :] for j in range(4)]
        grad = acc[4, at, :]
        sig = jax.nn.sigmoid(gate_pre)
        rest = sig * (1.0 - sig)
        first = sig + gate_pre * rest
        second = rest * (2.0 + gate_pre * (1.0 - 2.0 * sig))
        terms[0, at, :] = (grad * (second * gate_tan * up_pre + first * up_tan)).astype(
            jnp.bfloat16
        )
        terms[1, at, :] = (grad * first * gate_tan).astype(jnp.bfloat16)

    for i in range(3):
        pltpu.make_async_copy(raw.at[q], raw.at[q], raw_send.at[i]).wait()
        pltpu.make_async_copy(outbox.at[:, i], outbox.at[:, i], x_send.at[i]).wait()
    for i in range(2):
        whole = rows.at[:, :, core, r]
        pltpu.make_async_copy(whole, whole, ring_send.at[i]).wait()
        half = rows.at[:, i, core, r]
        pltpu.make_async_copy(half, half, half_send.at[i]).wait()
    for i in range(4):
        whole = rows.at[:, :, core, r]
        pltpu.make_async_copy(whole, whole, sib_send.at[i]).wait()
    pltpu.make_async_copy(rows.at[:, 0], xout, xout_sem).wait()


def back(terms, x, gate, up):
    out = jnp.dot(
        terms[...].reshape(-1, terms.shape[-1]),
        x[0].reshape(terms.shape[-1], -1),
        preferred_element_type=jnp.float32,
    ).astype(jnp.bfloat16)
    hidden = terms.shape[1]
    gate[0] = out[:hidden]
    up[0] = out[hidden:]


def local(tokens, cotangent, route_ids, gate_values, w_gate, w_up, w_down, d_gate, d_up):
    width = tokens.shape[1]
    hidden = w_down.shape[1]
    n = CHUNKS
    chunk = width // n
    by_hidden = [jnp.swapaxes(w[0], 0, 1) for w in (w_gate, w_up, d_gate, d_up)]
    block = (n, 2, 4, 4, 16, chunk)
    vmem = pl.BlockSpec(memory_space=pltpu.VMEM)
    hbm = pl.BlockSpec(memory_space=pl.ANY)
    dma = pltpu.SemaphoreType.DMA
    xs, terms = pl.pallas_call(
        front,
        out_shape=(
            jax.ShapeDtypeStruct(block, jnp.bfloat16),
            jax.ShapeDtypeStruct((2, hidden, 512), jnp.bfloat16),
        ),
        in_specs=[vmem] * 4 + [hbm] * 5,
        out_specs=(hbm, vmem),
        scratch_shapes=[
            pltpu.VMEM((4, 16, META + width), jnp.bfloat16),
            pltpu.VMEM((n, 4, 2, 16, chunk), jnp.bfloat16),
            pltpu.VMEM((n, 2, 2, 4, 4, 16, chunk), jnp.bfloat16),
            pltpu.VMEM((n, 5, hidden, chunk), jnp.bfloat16),
            pltpu.VMEM((5, hidden, 512), jnp.float32),
            dma((3,)),
            dma((n, 3)),
            dma((3,)),
            dma((n, 3)),
            dma((2,)),
            dma((n, 2)),
            dma((2,)),
            dma((n, 2)),
            dma((4,)),
            dma((n, 4)),
            dma((n,)),
            dma,
        ],
        compiler_params=pltpu.CompilerParams(
            collective_id=0, has_side_effects=True, vmem_limit_bytes=VMEM_LIMIT
        ),
        name="gather_and_project",
    )(tokens, cotangent, route_ids.T, gate_values.T, *by_hidden, w_down[0])

    out = jax.ShapeDtypeStruct((1, hidden, width), jnp.bfloat16)
    gate, up = pl.pallas_call(
        back,
        grid=(n,),
        out_shape=(out, out),
        in_specs=[
            pl.BlockSpec((2, hidden, 512), lambda i: (0, 0, 0)),
            pl.BlockSpec((1, 2, 4, 4, 16, chunk), lambda i: (i, 0, 0, 0, 0, 0)),
        ],
        out_specs=[pl.BlockSpec((1, hidden, chunk), lambda i: (0, 0, i))] * 2,
        compiler_params=pltpu.CompilerParams(vmem_limit_bytes=VMEM_LIMIT),
        name="outer_products",
    )(terms, xs)
    return jnp.swapaxes(gate, 1, 2), jnp.swapaxes(up, 1, 2)


def solution(mesh):
    rows = P(("dp", "expert"), None)
    columns = P("expert", None, "dp")
    return jax.shard_map(
        local,
        mesh=mesh,
        in_specs=(rows,) * 4 + (columns, columns, P("expert", "dp", None), columns, columns),
        out_specs=(columns, columns),
        check_vma=False,
    )
```

```python
import jax
import jax.numpy as jnp
from jax import lax
from jax.experimental import pallas as pl
from jax.experimental.pallas import tpu as pltpu
from jax.sharding import PartitionSpec as P

MESH = pl.DeviceIdType.MESH
NT = (((1,), (1,)), ((), ()))
TN = (((0,), (0,)), ((), ()))
META = 128
CHUNKS = (512, 1024, 1024, 1024, 512)
RAW_PIECES = (1, 1, 3)
FRONT_LIMIT = 40 * 2**20
BACK_LIMIT = 20 * 2**20
STEPS = (1, 3, 2)


def stay(array):
    return pltpu.with_memory_space_constraint(array, pltpu.HBM)


def offsets(sizes):
    return [sum(sizes[:k]) for k in range(len(sizes))]


def dispatch_matrix(ids, gates, x, ring):
    row = lax.broadcasted_iota(jnp.int32, (16, 128), 0)
    lane = lax.broadcasted_iota(jnp.int32, (16, 128), 1)
    expert = ((lane >> 5) + x) & 3
    kind = (lane >> 4) & 1
    here = (((lane >> 2) & 3) == ring) & ((row >> 3) == kind)
    slot = lane & 3
    taken = jnp.zeros((16, 128), jnp.int32)
    out = jnp.zeros((16, 128), jnp.float32)
    for t in range(ids.shape[1]):
        first = jnp.broadcast_to(ids[0:1, t : t + 1], (16, 128)) == expert
        second = jnp.broadcast_to(ids[1:2, t : t + 1], (16, 128)) == expert
        gate = jnp.where(
            first,
            jnp.broadcast_to(gates[0:1, t : t + 1], (16, 128)),
            jnp.broadcast_to(gates[1:2, t : t + 1], (16, 128)),
        )
        routed = first | second
        value = jnp.where(kind == 0, jnp.float32(1.0), gate)
        hit = routed & here & (taken == slot) & ((row & 7) == t)
        out = jnp.where(hit, value, out)
        taken = taken + routed.astype(jnp.int32)
    return out.astype(jnp.bfloat16)


def front(tok, cot, ids, gates, wg, wu, dg, du, wd, *refs):
    n = len(CHUNKS)
    rows, terms = refs[:n], refs[n]
    outbox = refs[n + 1 : 2 * n + 1]
    (
        raw,
        weights,
        acc,
        raw_send,
        raw_recv,
        x_send,
        x_recv,
        ring_send,
        ring_recv,
        half_send,
        half_recv,
        sib_send,
        sib_recv,
        w_sem,
        tok_in,
        cot_in,
        ids_in,
        gates_in,
        small_sem,
    ) = refs[2 * n + 1 :]
    at = offsets(CHUNKS)
    hidden, width = weights.shape[1:]

    small_copies = [
        pltpu.make_async_copy(src, dst, small_sem.at[i])
        for i, (src, dst) in enumerate(
            ((ids, ids_in), (gates, gates_in), (tok, tok_in), (cot, cot_in))
        )
    ]
    for copy in small_copies:
        copy.start()

    dp = lax.axis_index("dp")
    x = lax.axis_index("expert")
    y, z, core = dp // 8, (dp // 2) % 4, dp % 2
    q = jnp.where(core == 0, y, z)
    r = jnp.where(core == 0, z, y)

    def plane(q_at, r_at):
        q_at, r_at = lax.rem(q_at, 4), lax.rem(r_at, 4)
        y_at = jnp.where(core == 0, q_at, r_at)
        z_at = jnp.where(core == 0, r_at, q_at)
        return (y_at * 4 + z_at) * 2 + core

    raw_to = [(plane(q + d, r), x) for d in STEPS]
    x_to = [(dp, lax.rem(x + d, 4)) for d in STEPS]
    ring_to = [(plane(q, r + d), x) for d in (1, 3)]
    sibling = (dp + 1 - 2 * core, x)

    barrier = pltpu.get_barrier_semaphore()
    partners = raw_to + x_to + ring_to + [sibling]
    for device in partners:
        pl.semaphore_signal(barrier, inc=1, device_id=device, device_id_type=MESH)

    def remote(src, dst, send, recv, device):
        return pltpu.make_async_remote_copy(
            src_ref=src,
            dst_ref=dst,
            send_sem=send,
            recv_sem=recv,
            device_id=device,
            device_id_type=MESH,
        )

    raw[0] = jnp.zeros(raw.shape[1:], raw.dtype)
    for copy in small_copies:
        copy.wait()
    raw[0, 0:6, META:] = tok_in[...]
    raw[0, 8:14, META:] = cot_in[...]
    raw[0, :, 0:META] = dispatch_matrix(ids_in[...], gates_in[...].astype(jnp.float32), x, q)

    pl.semaphore_wait(barrier, len(partners))

    ends = [META + sum(CHUNKS[: sum(RAW_PIECES[: p + 1])]) for p in range(len(RAW_PIECES))]
    raw_copies = []
    for p, end in enumerate(ends):
        columns = slice(ends[p - 1] if p else 0, end)
        raw_copies.append(
            [
                remote(
                    raw.at[0, :, columns],
                    raw.at[d, :, columns],
                    raw_send.at[i],
                    raw_recv.at[p, i],
                    raw_to[i],
                )
                for i, d in enumerate(STEPS)
            ]
        )
    for copies in raw_copies:
        for copy in copies:
            copy.start()

    weight_copies = [
        pltpu.make_async_copy(w, weights.at[j], w_sem.at[j])
        for j, w in enumerate((wg, wu, dg, du, wd))
    ]
    for copy in weight_copies:
        copy.start()

    x_copies = [
        [
            remote(
                outbox[k].at[d],
                rows[k].at[:, 0, 0, d],
                x_send.at[i],
                x_recv.at[k, i],
                x_to[i],
            )
            for i, d in enumerate(STEPS)
        ]
        for k in range(n)
    ]
    ring_copies = [
        [
            remote(
                rows[k].at[:, 0, 0],
                rows[k].at[:, 0, 1 + i],
                ring_send.at[i],
                ring_recv.at[k, i],
                ring_to[i],
            )
            for i in range(2)
        ]
        for k in range(n)
    ]
    half_copies = [
        [
            remote(
                rows[k].at[i, 0, 1 + i],
                rows[k].at[i, 0, 3],
                half_send.at[i],
                half_recv.at[k, i],
                ring_to[i],
            )
            for i in range(2)
        ]
        for k in range(n)
    ]
    sib_copies = [
        [
            remote(
                rows[k].at[:, 0, part],
                rows[k].at[:, 1, part],
                sib_send.at[i],
                sib_recv.at[k, i],
                sibling,
            )
            for i, part in enumerate((slice(0, 3), slice(3, 4)))
        ]
        for k in range(n)
    ]

    def select(k):
        if k in offsets(RAW_PIECES):
            for copy in raw_copies[offsets(RAW_PIECES).index(k)]:
                copy.wait_recv()
        size = CHUNKS[k]
        blocks = raw[:, :, META + at[k] : META + at[k] + size].reshape(64, size)
        matrix = raw[:, :, 0:META].reshape(64, META)
        slots = lax.dot_general(matrix, blocks, TN, preferred_element_type=jnp.float32)
        slots = slots.astype(jnp.bfloat16).reshape(4, 2, 16, size)
        outbox[k][...] = slots
        for copy in x_copies[k]:
            copy.start()
        rows[k][:, 0, 0, 0] = slots[0]

    def exchange(k):
        for copy in x_copies[k]:
            copy.wait_recv()
        for copy in ring_copies[k]:
            copy.start()

    def forward(k):
        for copy in ring_copies[k]:
            copy.wait_recv()
        for copy in half_copies[k]:
            copy.start()
        sib_copies[k][0].start()

    def finish(k):
        for copy in half_copies[k]:
            copy.wait_recv()
        sib_copies[k][1].start()

    def arrive(k):
        for copy in sib_copies[k]:
            copy.wait_recv()

    def product(k, j):
        size = CHUNKS[k]
        if j == 0:
            arrive(k)
        if k == 0:
            weight_copies[j].wait()
        part = rows[k][j // 4].reshape(512, size)
        value = lax.dot_general(
            weights[j, :, at[k] : at[k] + size], part, NT, preferred_element_type=jnp.float32
        )
        if k == 0:
            acc[j] = value
        else:
            acc[j] += value

    pending = []

    def fill(count):
        for _ in range(min(count, len(pending))):
            product(*pending.pop(0))

    for i in range(n + 4):
        if i < n:
            select(i)
        fill(1)
        if 0 <= i - 1 < n:
            exchange(i - 1)
        fill(1)
        if 0 <= i - 2 < n:
            forward(i - 2)
        fill(2)
        if 0 <= i - 3 < n:
            finish(i - 3)
        fill(1)
        if 0 <= i - 3 < n:
            pending.extend((i - 3, j) for j in range(5))
    fill(len(pending))

    @pl.loop(0, hidden // 16)
    def _(b):
        block = pl.ds(pl.multiple_of(b * 16, 16), 16)
        gate_pre, up_pre, gate_tan, up_tan = [acc[j, block, :] for j in range(4)]
        grad = acc[4, block, :]
        sig = jax.nn.sigmoid(gate_pre)
        rest = sig * (1.0 - sig)
        first = sig + gate_pre * rest
        second = rest * (2.0 + gate_pre * (1.0 - 2.0 * sig))
        terms[0, block, :] = (grad * (second * gate_tan * up_pre + first * up_tan)).astype(
            jnp.bfloat16
        )
        terms[1, block, :] = (grad * first * gate_tan).astype(jnp.bfloat16)

    def sent(count, sem):
        whole = weights.at[0, 0:count]
        pltpu.make_async_copy(whole, whole, sem).wait()

    for i in range(3):
        pltpu.make_async_copy(raw.at[0], raw.at[0], raw_send.at[i]).wait()
        sent(32, x_send.at[i])
    for i in range(2):
        sent(128, ring_send.at[i])
        sent(64, half_send.at[i])
    sent(384, sib_send.at[0])
    sent(128, sib_send.at[1])


def back(*refs):
    n = len(CHUNKS)
    rows, terms = refs[:n], refs[n]
    gate, up = refs[n + 1 : n + 3]
    out, out_sem = refs[n + 3 : 2 * n + 3], refs[2 * n + 3]
    at = offsets(CHUNKS)
    out_copies = []
    for k, size in enumerate(CHUNKS):
        part = rows[k][0].reshape(512, size)
        for j, to in enumerate((gate, up)):
            out[k][j] = jnp.dot(terms[j], part, preferred_element_type=jnp.float32).astype(
                jnp.bfloat16
            )
            copy = pltpu.make_async_copy(
                out[k].at[j], to.at[0, :, at[k] : at[k] + size], out_sem.at[k, j]
            )
            copy.start()
            out_copies.append(copy)
    for copy in out_copies:
        copy.wait()


def local(tokens, cotangent, route_ids, gate_values, w_gate, w_up, w_down, d_gate, d_up):
    width = tokens.shape[1]
    hidden = w_down.shape[1]
    n = len(CHUNKS)
    by_hidden = [jnp.swapaxes(w[0], 0, 1) for w in (w_gate, w_up, d_gate, d_up)]
    vmem = pl.BlockSpec(memory_space=pltpu.VMEM)
    hbm = pl.BlockSpec(memory_space=pltpu.HBM)
    dma = pltpu.SemaphoreType.DMA
    bf16 = jnp.bfloat16
    blocks = [(2, 4, 4, 16, size) for size in CHUNKS]
    held = pl.pallas_call(
        front,
        out_shape=[pltpu.VMEM((2,) + block, bf16) for block in blocks]
        + [pltpu.VMEM((2, hidden, 512), bf16)],
        in_specs=[hbm] * 9,
        out_specs=[vmem] * (n + 1),
        scratch_shapes=[pltpu.VMEM((4, 2, 16, size), bf16) for size in CHUNKS]
        + [
            pltpu.VMEM((4, 16, META + width), bf16),
            pltpu.VMEM((5, hidden, width), bf16),
            pltpu.VMEM((5, hidden, 512), jnp.float32),
            dma((3,)),
            dma((len(RAW_PIECES), 3)),
            dma((3,)),
            dma((n, 3)),
            dma((2,)),
            dma((n, 2)),
            dma((2,)),
            dma((n, 2)),
            dma((2,)),
            dma((n, 2)),
            dma((5,)),
            pltpu.VMEM(tokens.shape, bf16),
            pltpu.VMEM(cotangent.shape, bf16),
            pltpu.VMEM(route_ids.shape[::-1], jnp.int32),
            pltpu.VMEM(gate_values.shape[::-1], bf16),
            dma((4,)),
        ],
        compiler_params=pltpu.CompilerParams(
            collective_id=0, has_side_effects=True, vmem_limit_bytes=FRONT_LIMIT
        ),
        name="gather_and_project",
    )(*map(stay, (tokens, cotangent, route_ids.T, gate_values.T, *by_hidden, w_down[0])))

    out = jax.ShapeDtypeStruct((1, hidden, width), bf16)
    gate, up = pl.pallas_call(
        back,
        out_shape=(out, out),
        in_specs=[vmem] * (n + 1),
        out_specs=[hbm] * 2,
        scratch_shapes=[pltpu.VMEM((2, hidden, size), bf16) for size in CHUNKS] + [dma((n, 2))],
        compiler_params=pltpu.CompilerParams(vmem_limit_bytes=BACK_LIMIT),
        name="outer_products",
    )(*held)
    return jnp.swapaxes(gate, 1, 2), jnp.swapaxes(up, 1, 2)


def solution(mesh):
    rows = P(("dp", "expert"), None)
    columns = P("expert", None, "dp")
    return jax.shard_map(
        local,
        mesh=mesh,
        in_specs=(rows,) * 4 + (columns, columns, P("expert", "dp", None), columns, columns),
        out_specs=(columns, columns),
        check_vma=False,
    )
```

```python
import jax
import jax.numpy as jnp
from jax import lax
from jax.experimental import pallas as pl
from jax.experimental.pallas import tpu as pltpu
from jax.sharding import PartitionSpec as P

MESH = pl.DeviceIdType.MESH
NT = (((1,), (1,)), ((), ()))
TN = (((0,), (0,)), ((), ()))
META = 128
CHUNKS = (512, 1024, 1024, 1024, 512)
RAW_PIECES = (1, 1, 3)
FRONT_LIMIT = 40 * 2**20
BACK_LIMIT = 20 * 2**20
STEPS = (1, 3, 2)


def stay(array):
    return pltpu.with_memory_space_constraint(array, pltpu.HBM)


def offsets(sizes):
    return [sum(sizes[:k]) for k in range(len(sizes))]


def dispatch_matrix(ids, gates, x, ring):
    row = lax.broadcasted_iota(jnp.int32, (16, 128), 0)
    lane = lax.broadcasted_iota(jnp.int32, (16, 128), 1)
    expert = ((lane >> 5) + x) & 3
    kind = (lane >> 4) & 1
    here = (((lane >> 2) & 3) == ring) & ((row >> 3) == kind)
    slot = lane & 3
    taken = jnp.zeros((16, 128), jnp.int32)
    out = jnp.zeros((16, 128), jnp.float32)
    for t in range(ids.shape[1]):
        first = jnp.broadcast_to(ids[0:1, t : t + 1], (16, 128)) == expert
        second = jnp.broadcast_to(ids[1:2, t : t + 1], (16, 128)) == expert
        gate = jnp.where(
            first,
            jnp.broadcast_to(gates[0:1, t : t + 1], (16, 128)),
            jnp.broadcast_to(gates[1:2, t : t + 1], (16, 128)),
        )
        routed = first | second
        value = jnp.where(kind == 0, jnp.float32(1.0), gate)
        hit = routed & here & (taken == slot) & ((row & 7) == t)
        out = jnp.where(hit, value, out)
        taken = taken + routed.astype(jnp.int32)
    return out.astype(jnp.bfloat16)


def front(tok, cot, ids, gates, wg, wu, dg, du, wd, *refs):
    n = len(CHUNKS)
    rows, terms = refs[:n], refs[n]
    outbox = refs[n + 1 : 2 * n + 1]
    (
        raw,
        weights,
        acc,
        raw_send,
        raw_recv,
        x_send,
        x_recv,
        ring_send,
        ring_recv,
        half_send,
        half_recv,
        sib_send,
        sib_recv,
        w_sem,
        tok_in,
        cot_in,
        ids_in,
        gates_in,
        small_sem,
    ) = refs[2 * n + 1 :]
    at = offsets(CHUNKS)
    hidden, width = weights.shape[1:]

    small_copies = [
        pltpu.make_async_copy(src, dst, small_sem.at[i])
        for i, (src, dst) in enumerate(
            ((ids, ids_in), (gates, gates_in), (tok, tok_in), (cot, cot_in))
        )
    ]
    for copy in small_copies:
        copy.start()

    dp = lax.axis_index("dp")
    x = lax.axis_index("expert")
    y, z, core = dp // 8, (dp // 2) % 4, dp % 2
    q = jnp.where(core == 0, y, z)
    r = jnp.where(core == 0, z, y)

    def plane(q_at, r_at):
        q_at, r_at = lax.rem(q_at, 4), lax.rem(r_at, 4)
        y_at = jnp.where(core == 0, q_at, r_at)
        z_at = jnp.where(core == 0, r_at, q_at)
        return (y_at * 4 + z_at) * 2 + core

    raw_to = [(plane(q + d, r), x) for d in STEPS]
    x_to = [(dp, lax.rem(x + d, 4)) for d in STEPS]
    ring_to = [(plane(q, r + d), x) for d in (1, 3, 2)]
    sibling = (dp + 1 - 2 * core, x)

    barrier = pltpu.get_barrier_semaphore()
    partners = raw_to + x_to + ring_to + [sibling]
    for device in partners:
        pl.semaphore_signal(barrier, inc=1, device_id=device, device_id_type=MESH)

    def remote(src, dst, send, recv, device):
        return pltpu.make_async_remote_copy(
            src_ref=src,
            dst_ref=dst,
            send_sem=send,
            recv_sem=recv,
            device_id=device,
            device_id_type=MESH,
        )

    raw[0] = jnp.zeros(raw.shape[1:], raw.dtype)
    for copy in small_copies:
        copy.wait()
    raw[0, 0:6, META:] = tok_in[...]
    raw[0, 8:14, META:] = cot_in[...]
    raw[0, :, 0:META] = dispatch_matrix(ids_in[...], gates_in[...].astype(jnp.float32), x, q)

    pl.semaphore_wait(barrier, len(partners))

    ends = [META + sum(CHUNKS[: sum(RAW_PIECES[: p + 1])]) for p in range(len(RAW_PIECES))]
    raw_copies = []
    for p, end in enumerate(ends):
        columns = slice(ends[p - 1] if p else 0, end)
        raw_copies.append(
            [
                remote(
                    raw.at[0, :, columns],
                    raw.at[d, :, columns],
                    raw_send.at[i],
                    raw_recv.at[p, i],
                    raw_to[i],
                )
                for i, d in enumerate(STEPS)
            ]
        )
    for copies in raw_copies:
        for copy in copies:
            copy.start()

    weight_copies = [
        pltpu.make_async_copy(w, weights.at[j], w_sem.at[j])
        for j, w in enumerate((wg, wu, dg, du, wd))
    ]
    for copy in weight_copies:
        copy.start()

    x_copies = [
        [
            remote(
                outbox[k].at[d],
                rows[k].at[:, 0, 0, d],
                x_send.at[i],
                x_recv.at[k, i],
                x_to[i],
            )
            for i, d in enumerate(STEPS)
        ]
        for k in range(n)
    ]
    ring_copies = [
        [
            remote(
                rows[k].at[:, 0, 0],
                rows[k].at[:, 0, 1 + i],
                ring_send.at[i],
                ring_recv.at[k, i],
                ring_to[i],
            )
            for i in range(3 if k == n - 1 else 2)
        ]
        for k in range(n)
    ]
    half_copies = [
        [
            remote(
                rows[k].at[i, 0, 1 + i],
                rows[k].at[i, 0, 3],
                half_send.at[i],
                half_recv.at[k, i],
                ring_to[i],
            )
            for i in range(2)
        ]
        for k in range(n - 1)
    ]
    sib_copies = [
        [
            remote(
                rows[k].at[:, 0, part],
                rows[k].at[:, 1, part],
                sib_send.at[i],
                sib_recv.at[k, i],
                sibling,
            )
            for i, part in enumerate((slice(0, 3), slice(3, 4)))
        ]
        for k in range(n - 1)
    ]
    sib_copies.append(
        [
            remote(
                rows[-1].at[:, 0],
                rows[-1].at[:, 1],
                sib_send.at[2],
                sib_recv.at[n - 1, 0],
                sibling,
            )
        ]
    )

    def select(k):
        if k in offsets(RAW_PIECES):
            for copy in raw_copies[offsets(RAW_PIECES).index(k)]:
                copy.wait_recv()
        size = CHUNKS[k]
        blocks = raw[:, :, META + at[k] : META + at[k] + size].reshape(64, size)
        matrix = raw[:, :, 0:META].reshape(64, META)
        slots = lax.dot_general(matrix, blocks, TN, preferred_element_type=jnp.float32)
        slots = slots.astype(jnp.bfloat16).reshape(4, 2, 16, size)
        outbox[k][...] = slots
        for copy in x_copies[k]:
            copy.start()
        rows[k][:, 0, 0, 0] = slots[0]

    def exchange(k):
        for copy in x_copies[k]:
            copy.wait_recv()
        for copy in ring_copies[k]:
            copy.start()

    def forward(k):
        for copy in ring_copies[k]:
            copy.wait_recv()
        if k < n - 1:
            for copy in half_copies[k]:
                copy.start()
        sib_copies[k][0].start()

    def finish(k):
        for copy in half_copies[k]:
            copy.wait_recv()
        sib_copies[k][1].start()

    def arrive(k):
        for copy in sib_copies[k]:
            copy.wait_recv()

    def product(k, owner, j):
        size = CHUNKS[k]
        if j == 0 and owner == 1:
            arrive(k)
        if k == 0 and owner == 0:
            weight_copies[j].wait()
        part = rows[k][j // 4, owner].reshape(256, size)
        value = lax.dot_general(
            weights[j, :, at[k] : at[k] + size], part, NT, preferred_element_type=jnp.float32
        )
        lanes = slice(owner * 256, owner * 256 + 256)
        if k == 0:
            acc[j, :, lanes] = value
        else:
            acc[j, :, lanes] += value

    def own(k):
        pending.extend((k, 0, j) for j in range(5))

    def other(k):
        pending.extend((k, 1, j) for j in range(5))

    pending = []

    def fill(count):
        for _ in range(min(count, len(pending))):
            product(*pending.pop(0))

    for i in range(n + 3):
        if i < n:
            select(i)
        fill(2)
        if 0 <= i - 1 < n:
            exchange(i - 1)
        fill(2)
        if 0 <= i - 2 < n:
            forward(i - 2)
            if i - 2 == n - 1:
                own(n - 1)
                other(n - 1)
        fill(4)
        if 0 <= i - 3 < n - 1:
            finish(i - 3)
            own(i - 3)
            other(i - 3)
        fill(2)
    fill(len(pending))

    @pl.loop(0, hidden // 16)
    def _(b):
        block = pl.ds(pl.multiple_of(b * 16, 16), 16)
        gate_pre, up_pre, gate_tan, up_tan = [acc[j, block, :] for j in range(4)]
        grad = acc[4, block, :]
        sig = jax.nn.sigmoid(gate_pre)
        rest = sig * (1.0 - sig)
        first = sig + gate_pre * rest
        second = rest * (2.0 + gate_pre * (1.0 - 2.0 * sig))
        terms[0, block, :] = (grad * (second * gate_tan * up_pre + first * up_tan)).astype(
            jnp.bfloat16
        )
        terms[1, block, :] = (grad * first * gate_tan).astype(jnp.bfloat16)

    def sent(count, sem, columns=width):
        whole = weights.at[0, 0:count, 0:columns]
        pltpu.make_async_copy(whole, whole, sem).wait()

    for i in range(3):
        pltpu.make_async_copy(raw.at[0], raw.at[0], raw_send.at[i]).wait()
        sent(32, x_send.at[i])
    for i in range(2):
        sent(128, ring_send.at[i])
        sent(64, half_send.at[i], at[-1])
    sent(384, sib_send.at[0], at[-1])
    sent(128, sib_send.at[1], at[-1])
    ring_copies[-1][2].wait_send()
    sib_copies[-1][0].wait_send()


def back(*refs):
    n = len(CHUNKS)
    rows, terms = refs[:n], refs[n]
    gate, up = refs[n + 1 : n + 3]
    out, out_sem = refs[n + 3 : 2 * n + 3], refs[2 * n + 3]
    at = offsets(CHUNKS)
    out_copies = []
    for k, size in enumerate(CHUNKS):
        part = rows[k][0].reshape(512, size)
        for j, to in enumerate((gate, up)):
            out[k][j] = jnp.dot(terms[j], part, preferred_element_type=jnp.float32).astype(
                jnp.bfloat16
            )
            copy = pltpu.make_async_copy(
                out[k].at[j], to.at[0, :, at[k] : at[k] + size], out_sem.at[k, j]
            )
            copy.start()
            out_copies.append(copy)
    for copy in out_copies:
        copy.wait()


def local(tokens, cotangent, route_ids, gate_values, w_gate, w_up, w_down, d_gate, d_up):
    width = tokens.shape[1]
    hidden = w_down.shape[1]
    n = len(CHUNKS)
    by_hidden = [jnp.swapaxes(w[0], 0, 1) for w in (w_gate, w_up, d_gate, d_up)]
    vmem = pl.BlockSpec(memory_space=pltpu.VMEM)
    hbm = pl.BlockSpec(memory_space=pltpu.HBM)
    dma = pltpu.SemaphoreType.DMA
    bf16 = jnp.bfloat16
    blocks = [(2, 4, 4, 16, size) for size in CHUNKS]
    held = pl.pallas_call(
        front,
        out_shape=[pltpu.VMEM((2,) + block, bf16) for block in blocks]
        + [pltpu.VMEM((2, hidden, 512), bf16)],
        in_specs=[hbm] * 9,
        out_specs=[vmem] * (n + 1),
        scratch_shapes=[pltpu.VMEM((4, 2, 16, size), bf16) for size in CHUNKS]
        + [
            pltpu.VMEM((4, 16, META + width), bf16),
            pltpu.VMEM((5, hidden, width), bf16),
            pltpu.VMEM((5, hidden, 512), jnp.float32),
            dma((3,)),
            dma((len(RAW_PIECES), 3)),
            dma((3,)),
            dma((n, 3)),
            dma((3,)),
            dma((n, 3)),
            dma((2,)),
            dma((n, 2)),
            dma((3,)),
            dma((n, 2)),
            dma((5,)),
            pltpu.VMEM(tokens.shape, bf16),
            pltpu.VMEM(cotangent.shape, bf16),
            pltpu.VMEM(route_ids.shape[::-1], jnp.int32),
            pltpu.VMEM(gate_values.shape[::-1], bf16),
            dma((4,)),
        ],
        compiler_params=pltpu.CompilerParams(
            collective_id=0, has_side_effects=True, vmem_limit_bytes=FRONT_LIMIT
        ),
        name="gather_and_project",
    )(*map(stay, (tokens, cotangent, route_ids.T, gate_values.T, *by_hidden, w_down[0])))

    out = jax.ShapeDtypeStruct((1, hidden, width), bf16)
    gate, up = pl.pallas_call(
        back,
        out_shape=(out, out),
        in_specs=[vmem] * (n + 1),
        out_specs=[hbm] * 2,
        scratch_shapes=[pltpu.VMEM((2, hidden, size), bf16) for size in CHUNKS] + [dma((n, 2))],
        compiler_params=pltpu.CompilerParams(vmem_limit_bytes=BACK_LIMIT),
        name="outer_products",
    )(*held)
    return jnp.swapaxes(gate, 1, 2), jnp.swapaxes(up, 1, 2)


def solution(mesh):
    rows = P(("dp", "expert"), None)
    columns = P("expert", None, "dp")
    return jax.shard_map(
        local,
        mesh=mesh,
        in_specs=(rows,) * 4 + (columns, columns, P("expert", "dp", None), columns, columns),
        out_specs=(columns, columns),
        check_vma=False,
    )
```

```python
import jax
import jax.numpy as jnp
from jax import lax
from jax.experimental import pallas as pl
from jax.experimental.pallas import tpu as pltpu
from jax.sharding import PartitionSpec as P

MESH = pl.DeviceIdType.MESH
NT = (((1,), (1,)), ((), ()))
TN = (((0,), (0,)), ((), ()))
META = 128
CHUNKS = (512, 1024, 1024, 1024, 512)
RAW_PIECES = (1, 1, 3)
FRONT_LIMIT = 40 * 2**20
BACK_LIMIT = 20 * 2**20
STEPS = (1, 3, 2)


def stay(array):
    return pltpu.with_memory_space_constraint(array, pltpu.HBM)


def offsets(sizes):
    return [sum(sizes[:k]) for k in range(len(sizes))]


def dispatch_matrix(ids, gates, x, ring):
    row = lax.broadcasted_iota(jnp.int32, (16, 128), 0)
    lane = lax.broadcasted_iota(jnp.int32, (16, 128), 1)
    expert = ((lane >> 5) + x) & 3
    kind = (lane >> 4) & 1
    here = (((lane >> 2) & 3) == ring) & ((row >> 3) == kind)
    slot = lane & 3
    taken = jnp.zeros((16, 128), jnp.int32)
    out = jnp.zeros((16, 128), jnp.float32)
    for t in range(ids.shape[1]):
        first = jnp.broadcast_to(ids[0:1, t : t + 1], (16, 128)) == expert
        second = jnp.broadcast_to(ids[1:2, t : t + 1], (16, 128)) == expert
        gate = jnp.where(
            first,
            jnp.broadcast_to(gates[0:1, t : t + 1], (16, 128)),
            jnp.broadcast_to(gates[1:2, t : t + 1], (16, 128)),
        )
        routed = first | second
        value = jnp.where(kind == 0, jnp.float32(1.0), gate)
        hit = routed & here & (taken == slot) & ((row & 7) == t)
        out = jnp.where(hit, value, out)
        taken = taken + routed.astype(jnp.int32)
    return out.astype(jnp.bfloat16)


def front(tok, cot, ids, gates, wg, wu, dg, du, wd, *refs):
    n = len(CHUNKS)
    rows, terms = refs[:n], refs[n]
    outbox = refs[n + 1 : 2 * n + 1]
    (
        raw,
        weights,
        acc,
        raw_send,
        raw_recv,
        x_send,
        x_recv,
        ring_send,
        ring_recv,
        half_send,
        half_recv,
        sib_send,
        sib_recv,
        w_sem,
        tok_in,
        cot_in,
        ids_in,
        gates_in,
        small_sem,
    ) = refs[2 * n + 1 :]
    at = offsets(CHUNKS)
    hidden, width = weights.shape[1:]

    small_copies = [
        pltpu.make_async_copy(src, dst, small_sem.at[i])
        for i, (src, dst) in enumerate(
            ((ids, ids_in), (gates, gates_in), (tok, tok_in), (cot, cot_in))
        )
    ]
    for copy in small_copies:
        copy.start()

    dp = lax.axis_index("dp")
    x = lax.axis_index("expert")
    y, z, core = dp // 8, (dp // 2) % 4, dp % 2
    q = jnp.where(core == 0, y, z)
    r = jnp.where(core == 0, z, y)

    def plane(q_at, r_at):
        q_at, r_at = lax.rem(q_at, 4), lax.rem(r_at, 4)
        y_at = jnp.where(core == 0, q_at, r_at)
        z_at = jnp.where(core == 0, r_at, q_at)
        return (y_at * 4 + z_at) * 2 + core

    raw_to = [(plane(q + d, r), x) for d in STEPS]
    x_to = [(dp, lax.rem(x + d, 4)) for d in STEPS]
    ring_to = [(plane(q, r + d), x) for d in (1, 3, 2)]
    sibling = (dp + 1 - 2 * core, x)

    barrier = pltpu.get_barrier_semaphore()
    partners = raw_to + x_to + ring_to + [sibling]
    for device in partners:
        pl.semaphore_signal(barrier, inc=1, device_id=device, device_id_type=MESH)

    def remote(src, dst, send, recv, device):
        return pltpu.make_async_remote_copy(
            src_ref=src,
            dst_ref=dst,
            send_sem=send,
            recv_sem=recv,
            device_id=device,
            device_id_type=MESH,
        )

    raw[0] = jnp.zeros(raw.shape[1:], raw.dtype)
    for copy in small_copies[:2]:
        copy.wait()
    raw[0, :, 0:META] = dispatch_matrix(ids_in[...], gates_in[...].astype(jnp.float32), x, q)
    for copy in small_copies[2:]:
        copy.wait()
    raw[0, 0:6, META:] = tok_in[...]
    raw[0, 8:14, META:] = cot_in[...]

    pl.semaphore_wait(barrier, len(partners))

    ends = [META + sum(CHUNKS[: sum(RAW_PIECES[: p + 1])]) for p in range(len(RAW_PIECES))]
    raw_copies = []
    for p, end in enumerate(ends):
        columns = slice(ends[p - 1] if p else 0, end)
        raw_copies.append(
            [
                remote(
                    raw.at[0, :, columns],
                    raw.at[d, :, columns],
                    raw_send.at[i],
                    raw_recv.at[p, i],
                    raw_to[i],
                )
                for i, d in enumerate(STEPS)
            ]
        )
    for copies in raw_copies:
        for copy in copies:
            copy.start()

    weight_copies = [
        pltpu.make_async_copy(w, weights.at[j], w_sem.at[j])
        for j, w in enumerate((wg, wu, dg, du, wd))
    ]
    for copy in weight_copies:
        copy.start()

    x_copies = [
        [
            remote(
                outbox[k].at[d],
                rows[k].at[:, 0, 0, d],
                x_send.at[i],
                x_recv.at[k, i],
                x_to[i],
            )
            for i, d in enumerate(STEPS)
        ]
        for k in range(n)
    ]
    ring_copies = [
        [
            remote(
                rows[k].at[:, 0, 0],
                rows[k].at[:, 0, 1 + i],
                ring_send.at[i],
                ring_recv.at[k, i],
                ring_to[i],
            )
            for i in range(3 if k == n - 1 else 2)
        ]
        for k in range(n)
    ]
    half_copies = [
        [
            remote(
                rows[k].at[i, 0, 1 + i],
                rows[k].at[i, 0, 3],
                half_send.at[i],
                half_recv.at[k, i],
                ring_to[i],
            )
            for i in range(2)
        ]
        for k in range(n - 1)
    ]
    sib_copies = [
        [
            remote(
                rows[k].at[:, 0, part],
                rows[k].at[:, 1, part],
                sib_send.at[i],
                sib_recv.at[k, i],
                sibling,
            )
            for i, part in enumerate((slice(0, 3), slice(3, 4)))
        ]
        for k in range(n - 1)
    ]
    sib_copies.append(
        [
            remote(
                rows[-1].at[:, 0],
                rows[-1].at[:, 1],
                sib_send.at[2],
                sib_recv.at[n - 1, 0],
                sibling,
            )
        ]
    )

    def select(k):
        if k in offsets(RAW_PIECES):
            for copy in raw_copies[offsets(RAW_PIECES).index(k)]:
                copy.wait_recv()
        size = CHUNKS[k]
        blocks = raw[:, :, META + at[k] : META + at[k] + size].reshape(64, size)
        matrix = raw[:, :, 0:META].reshape(64, META)
        slots = lax.dot_general(matrix, blocks, TN, preferred_element_type=jnp.float32)
        slots = slots.astype(jnp.bfloat16).reshape(4, 2, 16, size)
        outbox[k][...] = slots
        for copy in x_copies[k]:
            copy.start()
        rows[k][:, 0, 0, 0] = slots[0]

    def exchange(k):
        for copy in x_copies[k]:
            copy.wait_recv()
        for copy in ring_copies[k]:
            copy.start()

    def forward(k):
        for copy in ring_copies[k]:
            copy.wait_recv()
        if k < n - 1:
            for copy in half_copies[k]:
                copy.start()
        sib_copies[k][0].start()

    def finish(k):
        for copy in half_copies[k]:
            copy.wait_recv()
        sib_copies[k][1].start()

    def arrive(k):
        for copy in sib_copies[k]:
            copy.wait_recv()

    def product(k, owner, j):
        size = CHUNKS[k]
        if j == 0 and owner == 1:
            arrive(k)
        if k == 0 and owner == 0:
            weight_copies[j].wait()
        part = rows[k][j // 4, owner].reshape(256, size)
        value = lax.dot_general(
            weights[j, :, at[k] : at[k] + size], part, NT, preferred_element_type=jnp.float32
        )
        lanes = slice(owner * 256, owner * 256 + 256)
        if k == 0:
            acc[j, :, lanes] = value
        else:
            acc[j, :, lanes] += value

    def own(k):
        pending.extend((k, 0, j) for j in range(5))

    def other(k):
        pending.extend((k, 1, j) for j in range(5))

    pending = []

    def fill(count):
        for _ in range(min(count, len(pending))):
            product(*pending.pop(0))

    for i in range(n + 3):
        if i < n:
            select(i)
        fill(2)
        if 0 <= i - 1 < n:
            exchange(i - 1)
        fill(2)
        if 0 <= i - 2 < n:
            forward(i - 2)
            if i - 2 == n - 1:
                own(n - 1)
                other(n - 1)
        fill(4)
        if 0 <= i - 3 < n - 1:
            finish(i - 3)
            own(i - 3)
            other(i - 3)
        fill(2)
    fill(len(pending))

    @pl.loop(0, hidden // 16, unroll=2)
    def _(b):
        block = pl.ds(pl.multiple_of(b * 16, 16), 16)
        gate_pre, up_pre, gate_tan, up_tan = [acc[j, block, :] for j in range(4)]
        grad = acc[4, block, :]
        sig = jax.nn.sigmoid(gate_pre)
        rest = sig * (1.0 - sig)
        first = sig + gate_pre * rest
        second = rest * (2.0 + gate_pre * (1.0 - 2.0 * sig))
        terms[0, block, :] = (grad * (second * gate_tan * up_pre + first * up_tan)).astype(
            jnp.bfloat16
        )
        terms[1, block, :] = (grad * first * gate_tan).astype(jnp.bfloat16)

    def sent(count, sem, columns=width):
        whole = weights.at[0, 0:count, 0:columns]
        pltpu.make_async_copy(whole, whole, sem).wait()

    for i in range(3):
        pltpu.make_async_copy(raw.at[0], raw.at[0], raw_send.at[i]).wait()
        sent(32, x_send.at[i])
    for i in range(2):
        sent(128, ring_send.at[i])
        sent(64, half_send.at[i], at[-1])
    sent(384, sib_send.at[0], at[-1])
    sent(128, sib_send.at[1], at[-1])
    ring_copies[-1][2].wait_send()
    sib_copies[-1][0].wait_send()


def back(*refs):
    n = len(CHUNKS)
    rows, terms = refs[:n], refs[n]
    gate, up = refs[n + 1 : n + 3]
    out, out_sem = refs[n + 3 : 2 * n + 3], refs[2 * n + 3]
    at = offsets(CHUNKS)
    out_copies = []
    for k, size in enumerate(CHUNKS):
        part = rows[k][0].reshape(512, size)
        for j, to in enumerate((gate, up)):
            out[k][j] = jnp.dot(terms[j], part, preferred_element_type=jnp.float32).astype(
                jnp.bfloat16
            )
            copy = pltpu.make_async_copy(
                out[k].at[j], to.at[0, :, at[k] : at[k] + size], out_sem.at[k, j]
            )
            copy.start()
            out_copies.append(copy)
    for copy in out_copies:
        copy.wait()


def local(tokens, cotangent, route_ids, gate_values, w_gate, w_up, w_down, d_gate, d_up):
    width = tokens.shape[1]
    hidden = w_down.shape[1]
    n = len(CHUNKS)
    by_hidden = [jnp.swapaxes(w[0], 0, 1) for w in (w_gate, w_up, d_gate, d_up)]
    vmem = pl.BlockSpec(memory_space=pltpu.VMEM)
    hbm = pl.BlockSpec(memory_space=pltpu.HBM)
    dma = pltpu.SemaphoreType.DMA
    bf16 = jnp.bfloat16
    blocks = [(2, 4, 4, 16, size) for size in CHUNKS]
    held = pl.pallas_call(
        front,
        out_shape=[pltpu.VMEM((2,) + block, bf16) for block in blocks]
        + [pltpu.VMEM((2, hidden, 512), bf16)],
        in_specs=[hbm] * 9,
        out_specs=[vmem] * (n + 1),
        scratch_shapes=[pltpu.VMEM((4, 2, 16, size), bf16) for size in CHUNKS]
        + [
            pltpu.VMEM((4, 16, META + width), bf16),
            pltpu.VMEM((5, hidden, width), bf16),
            pltpu.VMEM((5, hidden, 512), jnp.float32),
            dma((3,)),
            dma((len(RAW_PIECES), 3)),
            dma((3,)),
            dma((n, 3)),
            dma((3,)),
            dma((n, 3)),
            dma((2,)),
            dma((n, 2)),
            dma((3,)),
            dma((n, 2)),
            dma((5,)),
            pltpu.VMEM(tokens.shape, bf16),
            pltpu.VMEM(cotangent.shape, bf16),
            pltpu.VMEM(route_ids.shape[::-1], jnp.int32),
            pltpu.VMEM(gate_values.shape[::-1], bf16),
            dma((4,)),
        ],
        compiler_params=pltpu.CompilerParams(
            collective_id=0, has_side_effects=True, vmem_limit_bytes=FRONT_LIMIT
        ),
        name="gather_and_project",
    )(*map(stay, (tokens, cotangent, route_ids.T, gate_values.T, *by_hidden, w_down[0])))

    out = jax.ShapeDtypeStruct((1, hidden, width), bf16)
    gate, up = pl.pallas_call(
        back,
        out_shape=(out, out),
        in_specs=[vmem] * (n + 1),
        out_specs=[hbm] * 2,
        scratch_shapes=[pltpu.VMEM((2, hidden, size), bf16) for size in CHUNKS] + [dma((n, 2))],
        compiler_params=pltpu.CompilerParams(vmem_limit_bytes=BACK_LIMIT),
        name="outer_products",
    )(*held)
    return jnp.swapaxes(gate, 1, 2), jnp.swapaxes(up, 1, 2)


def solution(mesh):
    rows = P(("dp", "expert"), None)
    columns = P("expert", None, "dp")
    return jax.shard_map(
        local,
        mesh=mesh,
        in_specs=(rows,) * 4 + (columns, columns, P("expert", "dp", None), columns, columns),
        out_specs=(columns, columns),
        check_vma=False,
    )
```
